512 devices in a mesh: row: 32 (over z, x), rep: 16 (over y, core).
Axes of the slice: x: 4, y: 8, z: 8, core: 2. Of those that a mesh axis runs over, the one named last changes fastest.
Arguments:
- features: bfloat16 [131072, 128], P('row'), may hold values from -6 to 6
- hub_local: int32 [32, 1], P('row'), may hold values from 0 to 31
- send_local: int32 [32, 16, 32, 2], P('row', 'rep'), may hold values from 0 to 31
- tile_rows: int32 [32, 16, 112], P('row', 'rep'), may hold values from 0 to 31
- tile_slots: int32 [32, 16, 112], P('row', 'rep'), may hold values from 0 to 95, as said below
- tile_values: bfloat16 [32, 16, 112, 128, 128], P('row', 'rep'), may hold values from -0.0625 to 0.0625
- weight: bfloat16 [128, 128], replicated, may hold values from -0.5 to 0.5
- out_bias: float32 [128], replicated, may hold values from -3 to 3
Outputs:
- hidden_out: bfloat16 [131072, 128], P(('row', 'rep'))
The draws below stay inside these ranges and needn't reach their ends.
Inputs may be any that keep to these rules, and one draw needn't show every extreme that they name: For every block and section, each slot of source appears in tile_slots at least once; the last 16 tiles of a section use hub slots.
All inputs are finite; a program needn't handle non-finite values.
Results may differ from the reference program's by a relative error of at most 0.0044.
Values may be sent and summed in bfloat16 or wider, within the bound.
A program may use at most 64 MiB of HBM per device.

```python
import jax
import jax.numpy as jnp
from jax import lax

F = 128
HID = 128
TILE = 128
FT = 32
HUB_DEV = 1
SPARSE = 2
EXTRA = 16
HUBS = 32
KT = 112
NODES = 131072
N_ROW = 32
N_REP = 16


def draw_tile_slots(key, part):
    key = jax.random.fold_in(key, 7)
    slot_total = HUB_DEV * N_ROW + N_ROW * SPARSE
    key_list = jax.random.split(key, N_ROW * N_REP)
    orderings = jax.vmap(lambda single: jax.random.permutation(single, slot_total))(key_list)
    hub_extra = jax.random.randint(jax.random.fold_in(key, 1), (N_ROW * N_REP, EXTRA), 0, HUB_DEV * N_ROW)
    joined = jnp.concatenate([orderings.astype(jnp.int32), hub_extra.astype(jnp.int32)], axis=1)
    return joined.reshape(N_ROW, N_REP, KT)


def place_ends(entries, own_key, least, largest):
    dims = entries.shape
    index_at = [jax.random.randint(jax.random.fold_in(own_key, axis), (), 0, dims[axis]) for axis in range(len(dims))]
    entries = entries.at[tuple(index_at)].set(least)
    longest = dims.index(max(dims))
    index_at[longest] = (index_at[longest] + 1) % dims[longest]
    return entries.at[tuple(index_at)].set(largest)


def steps_of(key, dims, pieces, low, largest):
    gain = 1.0
    for axis_at, blocks in pieces:
        draws = jax.random.uniform(jax.random.fold_in(jax.random.fold_in(key, 6), axis_at), (blocks,), jnp.float32, low / len(pieces), largest / len(pieces))
        gain = gain * jnp.repeat(jnp.exp(draws), dims[axis_at] // blocks).reshape((-1,) + (1,) * (len(dims) - 1 - axis_at))
    return gain


def centred(own_key, extent, deviation, most, shards=(), kind=jnp.bfloat16):
    drawn = jax.random.normal(own_key, extent, jnp.float32) * deviation
    if len(shards) > 0:
        drawn = steps_of(own_key, extent, shards, -0.22, 0.18) * drawn
    return jnp.clip(drawn, min=-most, max=most).astype(kind)


def setup_inputs(seed: int = 0) -> dict:
    streams_of = jax.random.split(jax.random.key(seed), 9)
    return {
        "features": centred(streams_of[0], (NODES, F), 1.0, 6.0, ((0, 32),)),
        "hub_local": place_ends(jax.random.randint(streams_of[1], (N_ROW, HUB_DEV), 0, FT), jax.random.fold_in(streams_of[1], 1), 0, FT - 1).astype(jnp.int32),
        "send_local": place_ends(jax.random.randint(streams_of[2], (N_ROW, N_REP, N_ROW, SPARSE), 0, FT), jax.random.fold_in(streams_of[2], 1), 0, FT - 1).astype(jnp.int32),
        "tile_rows": place_ends(jax.random.randint(streams_of[3], (N_ROW, N_REP, KT), 0, FT), jax.random.fold_in(streams_of[3], 1), 0, FT - 1).astype(jnp.int32),
        "tile_slots": draw_tile_slots(jax.random.fold_in(streams_of[8], 71), 0),
        "tile_values": centred(streams_of[5], (N_ROW, N_REP, KT, TILE, TILE), (TILE * KT * N_REP // FT) ** -0.5, 0.0625, ((0, 32), (1, 16))),
        "weight": centred(streams_of[6], (F, HID), F ** -0.5, 0.5),
        "out_bias": centred(streams_of[7], (HID,), 0.5, 3.0, (), jnp.float32),
    }


def section_partial(block_index, section_index, tile_grid, hub_tiles, send_local, tile_rows, tile_slots, tile_values):
    owners = jnp.arange(N_ROW, dtype=jnp.int32)[:, None]
    picks = send_local[:, section_index, block_index, :]
    sparse_tiles = tile_grid[owners, picks].reshape(N_ROW * SPARSE, TILE, F)
    source = jnp.concatenate([hub_tiles, sparse_tiles], axis=0)
    picked = source[tile_slots[block_index, section_index]]
    values = tile_values[block_index, section_index].astype(jnp.float32)
    products = jnp.einsum("kab,kbf->kaf", values, picked.astype(jnp.float32))
    return jax.ops.segment_sum(products, tile_rows[block_index, section_index], num_segments=FT)


def reference(features, hub_local, send_local, tile_rows, tile_slots, tile_values, weight, out_bias):
    tile_grid = features.reshape(N_ROW, FT, TILE, F)
    owners = jnp.arange(N_ROW, dtype=jnp.int32)[:, None]
    hub_tiles = tile_grid[owners, hub_local].reshape(HUBS, TILE, F)

    def per_block(block_index):
        def add_section(total, section_index):
            term = section_partial(block_index, section_index, tile_grid, hub_tiles, send_local, tile_rows, tile_slots, tile_values)
            return total + term, None

        start = jnp.zeros((FT, TILE, F), jnp.float32)
        total, _ = lax.scan(add_section, start, jnp.arange(N_REP, dtype=jnp.int32))
        return total

    sums = lax.map(per_block, jnp.arange(N_ROW, dtype=jnp.int32))
    aggregate = sums.reshape(NODES, F).astype(jnp.bfloat16)
    mixed = jnp.dot(aggregate, weight, preferred_element_type=jnp.float32) + out_bias
    return jax.nn.relu(mixed).astype(jnp.bfloat16)
```

```python
import functools

import jax
import jax.numpy as jnp
from jax import lax
from jax.experimental import pallas as pl
from jax.experimental.pallas import tpu as pltpu
from jax.sharding import PartitionSpec as P

F = 128
TILE = 128
NX = 4
NZ = 8
NY = 8
ROWS = 32
HUBS = 32
PIECE = 16
KT = 112
VMEM = pltpu.VMEM
MESH = pl.DeviceIdType.MESH


def zigzag(k, middle):
    return middle + (1 - 2 * (k % 2)) * ((k + 1) // 2)


def exchange_kernel(
    feat, hub, picks, out, outgoing, hub_mine, hub_got,
    hub_send, hub_recv, ring_send, ring_recv, tile_send, tile_recv, own_sem,
):
    r = lax.axis_index("row")
    q = lax.axis_index("rep")
    z, x = r // NX, r % NX
    y, c = q // 2, q % 2

    def partner(i):
        dz, dx = zigzag(i // NX, NZ // 2), zigzag(i % NX, NX // 2)
        return ((z + dz) % NZ) * NX + (x + dx) % NX

    def along_y(d):
        return ((y + d) % NY) * 2 + c

    barrier = pltpu.get_barrier_semaphore()

    def greet_row(i, carry):
        pl.semaphore_signal(barrier, inc=1, device_id=(partner(i), q), device_id_type=MESH)
        return carry

    def greet_y(d, carry):
        pl.semaphore_signal(barrier, inc=1, device_id=(r, along_y(d)), device_id_type=MESH)
        return carry

    lax.fori_loop(0, ROWS - 1, greet_row, 0)
    lax.fori_loop(1, NY, greet_y, 0)

    piece = pl.multiple_of(y * PIECE, PIECE)
    hub_mine[...] = feat[hub[0, 0]]
    hub_got[r] = hub_mine[pl.ds(piece, PIECE), :]
    pl.semaphore_wait(barrier, ROWS - 1 + NY - 1)

    def hub_copy(i):
        return pltpu.make_async_remote_copy(
            src_ref=hub_mine.at[pl.ds(piece, PIECE)], dst_ref=hub_got.at[r],
            send_sem=hub_send.at[i], recv_sem=hub_recv.at[i],
            device_id=(partner(i), q), device_id_type=MESH,
        )

    def tile_copy(i):
        return pltpu.make_async_remote_copy(
            src_ref=outgoing.at[i], dst_ref=out.at[pl.ds(HUBS + 2 * r, 2)],
            send_sem=tile_send.at[i], recv_sem=tile_recv.at[i],
            device_id=(partner(i), q), device_id_type=MESH,
        )

    def ring_copy(d):
        return pltpu.make_async_remote_copy(
            src_ref=hub_got, dst_ref=out.at[pl.ds(0, HUBS), pl.ds(piece, PIECE)],
            send_sem=ring_send.at[d], recv_sem=ring_recv.at[d],
            device_id=(r, along_y(d)), device_id_type=MESH,
        )

    def start_hub(i, carry):
        hub_copy(i).start()
        return carry

    lax.fori_loop(0, ROWS - 1, start_hub, 0)

    def gather(i):
        to = partner(i)
        for j in range(2):
            outgoing[i, j] = feat[picks[0, 0, to * 2 + j]]

    def start_tiles(i, carry):
        gather(i)
        tile_copy(i).start()
        return carry

    lax.fori_loop(0, ROWS - 1, start_tiles, 0)
    gather(ROWS - 1)
    own_tiles = pltpu.make_async_copy(
        outgoing.at[ROWS - 1], out.at[pl.ds(HUBS + 2 * r, 2)], own_sem.at[0]
    )
    own_tiles.start()

    def wait_hub(i, carry):
        hub_copy(i).wait()
        return carry

    lax.fori_loop(0, ROWS - 1, wait_hub, 0)
    own_hub = pltpu.make_async_copy(
        hub_got, out.at[pl.ds(0, HUBS), pl.ds(piece, PIECE)], own_sem.at[1]
    )
    own_hub.start()

    def start_ring(d, carry):
        ring_copy(d).start()
        return carry

    lax.fori_loop(1, NY, start_ring, 0)
    own_tiles.wait()
    own_hub.wait()

    def wait_ring(d, carry):
        ring_copy(d).wait()
        return carry

    lax.fori_loop(1, NY, wait_ring, 0)

    def wait_tiles(i, carry):
        tile_copy(i).wait()
        return carry

    lax.fori_loop(0, ROWS - 1, wait_tiles, 0)


def exchange(features, hub_local, picks):
    return pl.pallas_call(
        exchange_kernel,
        out_shape=jax.ShapeDtypeStruct((HUBS + 2 * ROWS, TILE, F), jnp.bfloat16),
        in_specs=[
            pl.BlockSpec(memory_space=VMEM),
            pl.BlockSpec(memory_space=pltpu.SMEM),
            pl.BlockSpec(memory_space=pltpu.SMEM),
        ],
        out_specs=pl.BlockSpec(memory_space=pl.ANY),
        scratch_shapes=[
            VMEM((ROWS, 2, TILE, F), jnp.bfloat16),
            VMEM((TILE, F), jnp.bfloat16),
            VMEM((ROWS, PIECE, F), jnp.bfloat16),
            pltpu.SemaphoreType.DMA((ROWS,)),
            pltpu.SemaphoreType.DMA((ROWS,)),
            pltpu.SemaphoreType.DMA((NY,)),
            pltpu.SemaphoreType.DMA((NY,)),
            pltpu.SemaphoreType.DMA((ROWS,)),
            pltpu.SemaphoreType.DMA((ROWS,)),
            pltpu.SemaphoreType.DMA((2,)),
        ],
        compiler_params=pltpu.CompilerParams(
            collective_id=0, has_side_effects=True, vmem_limit_bytes=32 * 1024 * 1024
        ),
        name="exchange",
    )(features, hub_local, picks)


STEP = 14


def product_kernel(tile_rows, tile_slots, values, source, total):
    step = pl.program_id(0)

    @pl.when(step == 0)
    def _():
        total[...] = jnp.zeros_like(total)

    for k in range(STEP):
        at = step * STEP + k
        start = pl.multiple_of(tile_rows[at] * TILE, TILE)
        total[pl.ds(start, TILE), :] += jnp.dot(
            values[k], source[tile_slots[at]], preferred_element_type=jnp.float32
        )


def products(tile_rows, tile_slots, values, source):
    return pl.pallas_call(
        product_kernel,
        out_shape=jax.ShapeDtypeStruct((ROWS * TILE, F), jnp.float32),
        grid_spec=pltpu.PrefetchScalarGridSpec(
            num_scalar_prefetch=2,
            grid=(KT // STEP,),
            in_specs=[
                pl.BlockSpec((STEP, TILE, TILE), lambda s, *_: (s, 0, 0)),
                pl.BlockSpec((HUBS + 2 * ROWS, TILE, F), lambda s, *_: (0, 0, 0)),
            ],
            out_specs=pl.BlockSpec((ROWS * TILE, F), lambda s, *_: (0, 0)),
        ),
        compiler_params=pltpu.CompilerParams(vmem_limit_bytes=32 * 1024 * 1024),
        name="products",
    )(tile_rows, tile_slots, values, source)


SHARE = 256


def reduce_kernel(
    part, weight, bias, out, core_got, outgoing, got,
    core_send, core_recv, send_sem, recv_sem,
):
    r = lax.axis_index("row")
    q = lax.axis_index("rep")
    y, c = q // 2, q % 2
    other = 1 - c

    def along_y(d):
        return ((y + d) % NY) * 2 + c

    barrier = pltpu.get_barrier_semaphore()
    pl.semaphore_signal(barrier, inc=1, device_id=(r, y * 2 + other), device_id_type=MESH)
    for d in range(1, NY):
        pl.semaphore_signal(barrier, inc=1, device_id=(r, along_y(d)), device_id_type=MESH)
    pl.semaphore_wait(barrier, NY)

    order = [zigzag(k, NY // 2) for k in range(NY)]
    across = []
    for d in order:
        to = (y + d) % NY
        copy = pltpu.make_async_remote_copy(
            src_ref=part.at[to, other], dst_ref=core_got.at[d],
            send_sem=core_send.at[d], recv_sem=core_recv.at[d],
            device_id=(r, y * 2 + other), device_id_type=MESH,
        )
        copy.start()
        across.append(copy)
    along = []
    for k, d in enumerate(order):
        across[k].wait()
        if d == 0:
            continue
        to = (y + d) % NY
        outgoing[d] = (part[to, c] + core_got[d]).astype(jnp.bfloat16)
        copy = pltpu.make_async_remote_copy(
            src_ref=outgoing.at[d], dst_ref=got.at[d],
            send_sem=send_sem.at[d], recv_sem=recv_sem.at[d],
            device_id=(r, along_y(d)), device_id_type=MESH,
        )
        copy.start()
        along.append(copy)
    total = part[y, c] + core_got[0]
    for copy in along[::-1]:
        copy.wait()
    for d in range(1, NY):
        total = total + got[d].astype(jnp.float32)
    aggregate = total.astype(jnp.bfloat16)
    mixed = jnp.dot(aggregate, weight[...], preferred_element_type=jnp.float32) + bias[...]
    out[...] = jnp.maximum(mixed, 0.0).astype(jnp.bfloat16)


def reduce_rows(part, weight, bias):
    return pl.pallas_call(
        reduce_kernel,
        out_shape=jax.ShapeDtypeStruct((SHARE, F), jnp.bfloat16),
        in_specs=[pl.BlockSpec(memory_space=VMEM)] * 3,
        out_specs=pl.BlockSpec(memory_space=VMEM),
        scratch_shapes=[
            VMEM((NY, SHARE, F), jnp.float32),
            VMEM((NY, SHARE, F), jnp.bfloat16),
            VMEM((NY, SHARE, F), jnp.bfloat16),
            pltpu.SemaphoreType.DMA((NY,)),
            pltpu.SemaphoreType.DMA((NY,)),
            pltpu.SemaphoreType.DMA((NY,)),
            pltpu.SemaphoreType.DMA((NY,)),
        ],
        compiler_params=pltpu.CompilerParams(
            collective_id=1, has_side_effects=True, vmem_limit_bytes=32 * 1024 * 1024
        ),
        name="reduce_rows",
    )(part, weight, bias)


def local(features, hub_local, send_local, tile_rows, tile_slots, tile_values, weight, out_bias):
    source = exchange(features.reshape(ROWS, TILE, F), hub_local, send_local.reshape(1, 1, 2 * ROWS))
    part = products(tile_rows.reshape(KT), tile_slots.reshape(KT), tile_values[0, 0], source)
    return reduce_rows(part.reshape(NY, 2, SHARE, F), weight, out_bias.reshape(1, F))


def solution(mesh):
    placed = (
        P("row", None),
        P("row", None),
        P("row", "rep", None, None),
        P("row", "rep", None),
        P("row", "rep", None),
        P("row", "rep", None, None, None),
        P(),
        P(),
    )
    return jax.shard_map(
        local, mesh=mesh, in_specs=placed, out_specs=P(("row", "rep"), None), check_vma=False
    )
```

```python
import functools

import jax
import jax.numpy as jnp
from jax import lax
from jax.experimental import pallas as pl
from jax.experimental.pallas import tpu as pltpu
from jax.sharding import PartitionSpec as P

F = 128
TILE = 128
NX = 4
NZ = 8
NY = 8
ROWS = 32
HUBS = 32
PIECE = 16
KT = 112
VMEM = pltpu.VMEM
MESH = pl.DeviceIdType.MESH


def zigzag(k, middle):
    return middle + (1 - 2 * (k % 2)) * ((k + 1) // 2)


FAR = (4,)
NEAR = 28
CLASS = 16
HUB_ITEM = len(FAR)


def exchange_kernel(
    features, hub, picks, picks_far, out,
    feat, outgoing, hub_tile, hub_got, far_0, far_out, picks_got, picks_at,
    feat_sem, own_sem, near_send, near_recv, hub_send, hub_recv, far_send, far_recv,
    pick_send, pick_recv, pick_sem, ring_send, ring_recv,
    core_send, core_recv, last_send, last_recv,
):
    far = (far_0,)
    r = lax.axis_index("row")
    q = lax.axis_index("rep")
    z, x = lax.div(r, NX), lax.rem(r, NX)
    y, c = lax.div(q, 2), lax.rem(q, 2)
    kind = lax.rem(z + c, 2)
    half_z = lax.div(z, 2)
    other = q + 1 - 2 * c
    layer = [z] + [lax.rem(z + d, NZ) for d in range(1, NZ)]
    line = [lax.rem(x + d, NX) for d in range(NX)]
    first_row = [at * NX for at in layer]
    place = [y] + [lax.rem(y + d, NY) for d in range(1, NY)]
    shares = [at * 4 + 2 * c for at in place]
    pieces = [pl.multiple_of(at * PIECE, PIECE) for at in place]

    def remote(src, dst, send, recv, row, rep):
        return pltpu.make_async_remote_copy(
            src_ref=src, dst_ref=dst, send_sem=send, recv_sem=recv,
            device_id=(row, rep), device_id_type=MESH,
        )

    load = pltpu.make_async_copy(features, feat, feat_sem)
    load.start()

    barrier = pltpu.get_barrier_semaphore()

    def greet(row, rep):
        pl.semaphore_signal(barrier, inc=1, device_id=(row, rep), device_id_type=MESH)

    for dz in range(NZ):
        for dx in range(NX):
            if dz or dx:
                greet(first_row[dz] + line[dx], q)
    for rep in (*(place[d] * 2 + c for d in (1, 2, 6, 7)), other):
        greet(r, rep)

    load.wait()
    hub_tile[...] = feat[hub[0, 0]]

    @pl.when(c == 0)
    def _():
        hub_got[half_z, x] = hub_tile[pl.ds(pieces[0], PIECE), :]

    pl.semaphore_wait(barrier, ROWS - 1 + 5)

    slot_line, slot_first = lax.div(x, 2), 2 * lax.rem(x, 2)

    def slot(at):
        return out.at[HUBS // 8 + at, slot_line, pl.ds(slot_first, 2)]

    my_slot = slot(z)

    def hub_copy(i):
        row = lax.rem(z + 2 * lax.div(i, NX) + c, NZ) * NX + lax.rem(x + lax.rem(i, NX), NX)
        return remote(
            hub_tile.at[pl.ds(pieces[0], PIECE)], hub_got.at[half_z, x],
            hub_send.at[i], hub_recv.at[i], row, q,
        )

    def start_hub(i, carry):
        hub_copy(i).start()
        return carry

    lax.fori_loop(1 - c, CLASS, start_hub, 0)
    far_copy, pick_copy = [], []
    for b, dz in enumerate(FAR):
        far_copy.append(remote(
            feat.at[pl.ds(shares[0], 2)], far[b].at[pl.ds(shares[0], 2)],
            far_send.at[b], far_recv.at[b], first_row[dz] + x, q,
        ))
        pick_copy.append(remote(
            picks_far.at[layer[dz]], picks_got.at[b],
            pick_send.at[b], pick_recv.at[b], first_row[dz] + x, q,
        ))
        far_copy[b].start()
        pick_copy[b].start()

    near_copy = []
    for dz in (3, 5, 2, 6, 1, 7, 0):
        for dx in (2, 1, 3, 0):
            i = len(near_copy)
            row = first_row[dz] + line[dx]
            at = row * 2
            for j in range(2):
                outgoing[i, j] = feat[picks[0, 0, at + j]]
            if dz or dx:
                copy = remote(
                    outgoing.at[i], my_slot, near_send.at[i], near_recv.at[i], row, q
                )
            else:
                copy = pltpu.make_async_copy(outgoing.at[i], my_slot, own_sem.at[0])
            copy.start()
            near_copy.append(copy)

    def chunk(b, dy, first, count):
        if b == HUB_ITEM:
            return out.at[pl.ds(2 * first, 2 * count), kind, :, pl.ds(pieces[dy], PIECE)]
        return far[b].at[pl.ds(shares[dy] + first if first else shares[dy], count)]

    def mine(b):
        return hub_got if b == HUB_ITEM else chunk(b, 0, 0, 2)

    ring_copies, core_copies = {}, {}

    def start_ring(b, dy, way, first=0, count=2):
        at = len(ring_copies.setdefault(b, []))
        copy = remote(
            chunk(b, dy, first, count) if dy else mine(b), chunk(b, dy, first, count),
            ring_send.at[b, at], ring_recv.at[b, at], r, place[way % NY] * 2 + c,
        )
        copy.start()
        ring_copies[b].append(copy)

    def start_core(b, dy, first=0, count=2):
        at = len(core_copies.setdefault(b, []))
        copy = remote(
            chunk(b, dy, first, count) if dy else mine(b), chunk(b, dy, first, count),
            core_send.at[b, at], core_recv.at[b, at], r, other,
        )
        copy.start()
        core_copies[b].append(copy)

    own_hub = pltpu.make_async_copy(hub_got, chunk(HUB_ITEM, 0, 0, 2), own_sem.at[1])
    to_scalar = [
        pltpu.make_async_copy(picks_got.at[b], picks_at.at[b], pick_sem.at[b])
        for b in range(len(FAR))
    ]

    def spread(b):
        if b == HUB_ITEM:

            def wait_hub(i, carry):
                hub_copy(i).wait()
                return carry

            lax.fori_loop(1 - c, CLASS, wait_hub, 0)
        else:
            far_copy[b].wait()
        for way in (2, -2, 1, -1):
            start_ring(b, 0, way)
        start_core(b, 0)
        if b == HUB_ITEM:
            own_hub.start()
        else:
            pick_copy[b].wait()
            to_scalar[b].start()

    def spread_on(b):
        for at, way in enumerate((2, -2)):
            ring_copies[b][at].wait_recv()
            on = way // 2
            start_ring(b, -way % NY, way, 0 if on > 0 else 1, 1)
            start_ring(b, -way % NY, on)
            start_core(b, -way % NY)
        for at, way in ((2, 1), (3, -1)):
            ring_copies[b][at].wait_recv()
            start_core(b, -way % NY)

    def collect(b):
        for at, way in ((5, 3), (7, -3)):
            ring_copies[b][at].wait_recv()
            start_core(b, -way % NY)
        for at, first in ((4, 0), (6, 1)):
            ring_copies[b][at].wait_recv()
            start_core(b, NY // 2, first, 1)

    last_copy = []

    def pass_on(b):
        to_scalar[b].wait()
        dst = slot(layer[NZ - FAR[b]])
        for k, dx in enumerate((2, 1, 3, 0)):
            at = line[dx] * 2
            for j in range(2):
                far_out[b, k, j] = far[b][picks_at[b, 0, at + j]]
            if dx:
                copy = remote(
                    far_out.at[b, k], dst, last_send.at[b, k], last_recv.at[b, k],
                    first_row[0] + line[dx], q,
                )
            else:
                copy = pltpu.make_async_copy(far_out.at[b, k], dst, own_sem.at[2 + b])
            copy.start()
            last_copy.append(copy)

    for b in range(len(FAR)):
        spread(b)
    spread(HUB_ITEM)
    for b in range(len(FAR)):
        spread_on(b)
    spread_on(HUB_ITEM)
    for b in range(len(FAR)):
        collect(b)
        for copy in core_copies[b]:
            copy.wait()
        pass_on(b)
    collect(HUB_ITEM)
    for copy in core_copies[HUB_ITEM]:
        copy.wait()

    for copies in ring_copies.values():
        for copy in copies:
            copy.wait_send()
    own_hub.wait()
    for copy in near_copy + last_copy:
        copy.wait()


def exchange(features, hub_local, picks):
    dma = pltpu.SemaphoreType.DMA
    far = len(FAR)
    picks_far = jnp.pad(picks.reshape(NZ, 1, 2 * NX), ((0, 0), (0, 7), (0, 128 - 2 * NX)))
    return pl.pallas_call(
        exchange_kernel,
        out_shape=jax.ShapeDtypeStruct((12, 2, 4, TILE, F), jnp.bfloat16),
        in_specs=[
            pl.BlockSpec(memory_space=pl.ANY),
            pl.BlockSpec(memory_space=pltpu.SMEM),
            pl.BlockSpec(memory_space=pltpu.SMEM),
            pl.BlockSpec(memory_space=VMEM),
        ],
        out_specs=pl.BlockSpec(memory_space=pl.ANY),
        scratch_shapes=[
            VMEM((ROWS, TILE, F), jnp.bfloat16),
            VMEM((NEAR, 2, TILE, F), jnp.bfloat16),
            VMEM((TILE, F), jnp.bfloat16),
            VMEM((4, 4, PIECE, F), jnp.bfloat16),
            *[VMEM((ROWS, TILE, F), jnp.bfloat16)] * far,
            VMEM((far, NX, 2, TILE, F), jnp.bfloat16),
            VMEM((far, 8, 128), jnp.int32),
            pltpu.SMEM((far, 8, 128), jnp.int32),
            dma(()),
            dma((2 + far,)),
            dma((NEAR,)),
            dma((NEAR,)),
            dma((CLASS,)),
            dma((CLASS,)),
            dma((far,)),
            dma((far,)),
            dma((far,)),
            dma((far,)),
            dma((far,)),
            dma((far + 1, 8)),
            dma((far + 1, 8)),
            dma((far + 1, 9)),
            dma((far + 1, 9)),
            dma((far, NX)),
            dma((far, NX)),
        ],
        compiler_params=pltpu.CompilerParams(
            collective_id=0, has_side_effects=True, vmem_limit_bytes=32 * 1024 * 1024
        ),
        name="exchange",
    )(features, hub_local, picks, picks_far)


STEP = 14


def product_kernel(tile_rows, tile_slots, values, source, total):
    step = pl.program_id(0)

    @pl.when(step == 0)
    def _():
        total[...] = jnp.zeros_like(total)

    for k in range(STEP):
        at = step * STEP + k
        start = pl.multiple_of(tile_rows[at] * TILE, TILE)
        total[pl.ds(start, TILE), :] += jnp.dot(
            values[k], source[tile_slots[at]], preferred_element_type=jnp.float32
        )


def products(tile_rows, tile_slots, values, source):
    return pl.pallas_call(
        product_kernel,
        out_shape=jax.ShapeDtypeStruct((ROWS * TILE, F), jnp.float32),
        grid_spec=pltpu.PrefetchScalarGridSpec(
            num_scalar_prefetch=2,
            grid=(KT // STEP,),
            in_specs=[
                pl.BlockSpec((STEP, TILE, TILE), lambda s, *_: (s, 0, 0)),
                pl.BlockSpec((HUBS + 2 * ROWS, TILE, F), lambda s, *_: (0, 0, 0)),
            ],
            out_specs=pl.BlockSpec((ROWS * TILE, F), lambda s, *_: (0, 0)),
        ),
        compiler_params=pltpu.CompilerParams(vmem_limit_bytes=32 * 1024 * 1024),
        name="products",
    )(tile_rows, tile_slots, values, source)


SHARE = 256


def reduce_kernel(
    part, weight, bias, out, core_got, outgoing, got,
    core_send, core_recv, send_sem, recv_sem,
):
    r = lax.axis_index("row")
    q = lax.axis_index("rep")
    y, c = q // 2, q % 2
    other = 1 - c

    def along_y(d):
        return ((y + d) % NY) * 2 + c

    barrier = pltpu.get_barrier_semaphore()
    pl.semaphore_signal(barrier, inc=1, device_id=(r, y * 2 + other), device_id_type=MESH)
    for d in range(1, NY):
        pl.semaphore_signal(barrier, inc=1, device_id=(r, along_y(d)), device_id_type=MESH)
    pl.semaphore_wait(barrier, NY)

    order = [zigzag(k, NY // 2) for k in range(NY)]
    across = []
    for d in order:
        to = (y + d) % NY
        copy = pltpu.make_async_remote_copy(
            src_ref=part.at[to, other], dst_ref=core_got.at[d],
            send_sem=core_send.at[d], recv_sem=core_recv.at[d],
            device_id=(r, y * 2 + other), device_id_type=MESH,
        )
        copy.start()
        across.append(copy)
    along = []
    for k, d in enumerate(order):
        across[k].wait()
        if d == 0:
            continue
        to = (y + d) % NY
        outgoing[d] = (part[to, c] + core_got[d]).astype(jnp.bfloat16)
        copy = pltpu.make_async_remote_copy(
            src_ref=outgoing.at[d], dst_ref=got.at[d],
            send_sem=send_sem.at[d], recv_sem=recv_sem.at[d],
            device_id=(r, along_y(d)), device_id_type=MESH,
        )
        copy.start()
        along.append(copy)
    total = part[y, c] + core_got[0]
    for copy in along[::-1]:
        copy.wait()
    for d in range(1, NY):
        total = total + got[d].astype(jnp.float32)
    aggregate = total.astype(jnp.bfloat16)
    mixed = jnp.dot(aggregate, weight[...], preferred_element_type=jnp.float32) + bias[...]
    out[...] = jnp.maximum(mixed, 0.0).astype(jnp.bfloat16)


def reduce_rows(part, weight, bias):
    return pl.pallas_call(
        reduce_kernel,
        out_shape=jax.ShapeDtypeStruct((SHARE, F), jnp.bfloat16),
        in_specs=[pl.BlockSpec(memory_space=VMEM)] * 3,
        out_specs=pl.BlockSpec(memory_space=VMEM),
        scratch_shapes=[
            VMEM((NY, SHARE, F), jnp.float32),
            VMEM((NY, SHARE, F), jnp.bfloat16),
            VMEM((NY, SHARE, F), jnp.bfloat16),
            pltpu.SemaphoreType.DMA((NY,)),
            pltpu.SemaphoreType.DMA((NY,)),
            pltpu.SemaphoreType.DMA((NY,)),
            pltpu.SemaphoreType.DMA((NY,)),
        ],
        compiler_params=pltpu.CompilerParams(
            collective_id=1, has_side_effects=True, vmem_limit_bytes=32 * 1024 * 1024
        ),
        name="reduce_rows",
    )(part, weight, bias)


def local(features, hub_local, send_local, tile_rows, tile_slots, tile_values, weight, out_bias):
    source = exchange(features.reshape(ROWS, TILE, F), hub_local, send_local.reshape(1, 1, 2 * ROWS))
    part = products(tile_rows.reshape(KT), tile_slots.reshape(KT), tile_values[0, 0], source.reshape(HUBS + 2 * ROWS, TILE, F))
    return reduce_rows(part.reshape(NY, 2, SHARE, F), weight, out_bias.reshape(1, F))


def solution(mesh):
    placed = (
        P("row", None),
        P("row", None),
        P("row", "rep", None, None),
        P("row", "rep", None),
        P("row", "rep", None),
        P("row", "rep", None, None, None),
        P(),
        P(),
    )
    return jax.shard_map(
        local, mesh=mesh, in_specs=placed, out_specs=P(("row", "rep"), None), check_vma=False
    )
```

```python
import functools

import jax
import jax.numpy as jnp
from jax import lax
from jax.experimental import pallas as pl
from jax.experimental.pallas import tpu as pltpu
from jax.sharding import PartitionSpec as P

F = 128
TILE = 128
NX = 4
NZ = 8
NY = 8
ROWS = 32
HUBS = 32
PIECE = 16
KT = 112
VMEM = pltpu.VMEM
MESH = pl.DeviceIdType.MESH


def zigzag(k, middle):
    return middle + (1 - 2 * (k % 2)) * ((k + 1) // 2)


FAR = 4
NEAR_Z = (3, 5, 2, 6, 1, 7, 0)
LINE = (2, 1, 3, 0)
NEAR = len(NEAR_Z) * NX
CLASS = 16
FAR_ITEM, HUB_ITEM = 0, 1
EMPTY = KT
SHARE = 256
HALF = F // 2
ORDER = tuple(zigzag(k, NY // 2) for k in range(NY))
UNROLL = 8


def halves(one, two):
    return (
        jnp.concatenate([one[:, :HALF], two[:, :HALF]], axis=1),
        jnp.concatenate([one[:, HALF:], two[:, HALF:]], axis=1),
    )


def layer_kernel(
    features, hub, picks, picks_far, rows_at, rows_in, slots, values, weight, bias, out,
    feat, tiles, outgoing, hub_tile, hub_got, far, far_out, picks_got, picks_at,
    source_0, source_1, linked, links, sums, part_own, part_other, core_got, sum_out, sum_got,
    load_sem, scalar_sem, near_send, near_recv, hub_send, hub_recv, far_send, far_recv,
    ring_send, ring_recv, core_send, core_recv, last_send, last_recv,
    cross_send, cross_recv, sum_send, sum_recv,
):
    source = (source_0, source_1)
    r = lax.axis_index("row")
    q = lax.axis_index("rep")
    z, x = lax.div(r, NX), lax.rem(r, NX)
    y, c = lax.div(q, 2), lax.rem(q, 2)
    kind = lax.rem(z + c, 2)
    half_z, odd_z = lax.div(z, 2), lax.rem(z, 2)
    other = q + 1 - 2 * c
    layer = [z] + [lax.rem(z + d, NZ) for d in range(1, NZ)]
    line = [lax.rem(x + d, NX) for d in range(NX)]
    first_row = [at * NX for at in layer]
    place = [y] + [lax.rem(y + d, NY) for d in range(1, NY)]
    shares = [at * 4 + 2 * c for at in place]
    pieces = [pl.multiple_of(at * PIECE, PIECE) for at in place]
    along = [at * 2 + c for at in place]

    def remote(src, dst, send, recv, row, rep):
        return pltpu.make_async_remote_copy(
            src_ref=src, dst_ref=dst, send_sem=send, recv_sem=recv,
            device_id=(row, rep), device_id_type=MESH,
        )

    load = pltpu.make_async_copy(features, feat, load_sem.at[0])
    load.start()
    load_tiles = pltpu.make_async_copy(values, tiles, load_sem.at[1])
    load_tiles.start()

    barrier = pltpu.get_barrier_semaphore()

    def greet(row, rep):
        pl.semaphore_signal(barrier, inc=1, device_id=(row, rep), device_id_type=MESH)

    for dz in range(NZ):
        for dx in range(NX):
            if dz or dx:
                greet(first_row[dz] + line[dx], q)
    for rep in (*along[1:], other):
        greet(r, rep)

    load.wait()
    hub_tile[...] = feat[hub[0, 0]]

    @pl.when(c == 0)
    def _():
        hub_got[half_z, x] = hub_tile[pl.ds(pieces[0], PIECE), :]

    pl.semaphore_wait(barrier, ROWS - 1 + NY)

    def hub_copy(i):
        row = lax.rem(z + 2 * lax.div(i, NX) + c, NZ) * NX + lax.rem(x + lax.rem(i, NX), NX)
        return remote(
            hub_tile.at[pl.ds(pieces[0], PIECE)], hub_got.at[half_z, x],
            hub_send.at[i], hub_recv.at[i], row, q,
        )

    def start_hub(i, carry):
        hub_copy(i).start()
        return carry

    lax.fori_loop(1 - c, CLASS, start_hub, 0)
    far_row = first_row[FAR] + x
    far_copy = remote(
        feat.at[pl.ds(shares[0], 2)], far.at[pl.ds(shares[0], 2)],
        far_send.at[0], far_recv.at[0], far_row, q,
    )
    pick_copy = remote(
        picks_far, picks_got, far_send.at[1], far_recv.at[1], far_row, q
    )
    far_copy.start()
    pick_copy.start()

    near_copy = ([], [])
    for dz in NEAR_Z:
        for dx in LINE:
            i = len(near_copy[0])
            row = first_row[dz] + line[dx]
            pair = halves(feat[picks[0, row]], feat[picks[1, row]])
            if dz == 0 and dx == 0:
                for h in range(2):
                    source[h][4 + half_z, odd_z, x] = pair[h]
                continue
            for h in range(2):
                outgoing[i, h] = pair[h]
                near_copy[h].append(remote(
                    outgoing.at[i, h], source[h].at[4 + half_z, odd_z, x],
                    near_send.at[h, i], near_recv.at[h, i], row, q,
                ))
            near_copy[0][i].start()

    def second_half(first, last):
        for i in range(first, last):
            near_copy[0][i].wait_send()
            near_copy[1][i].start()

    lane = lax.broadcasted_iota(jnp.int32, (1, KT), 1)
    rows_lane = rows_in[...]

    def link(j, carry):
        before, final = carry
        row = rows_at[0, 0, j]
        before = jnp.where((rows_lane == row) & (lane > j), j, before)
        final = jnp.where(lane == row, j, final)
        return before, final

    none = jnp.full((1, KT), EMPTY, jnp.int32)
    before, final = lax.fori_loop(0, KT, link, (none, none))
    linked[...] = jnp.zeros((8, 128), jnp.int32)
    linked[pl.ds(0, 1), pl.ds(0, KT)] = before
    linked[pl.ds(1, 1), pl.ds(0, KT)] = final
    to_links = pltpu.make_async_copy(linked, links, scalar_sem.at[0])
    to_links.start()

    def chunk(b, dy, first, count):
        if b == HUB_ITEM:
            return source_0.at[pl.ds(2 * first, 2 * count), kind, :, pl.ds(pieces[dy], PIECE)]
        return far.at[pl.ds(shares[dy] + first if first else shares[dy], count)]

    def mine(b):
        return hub_got if b == HUB_ITEM else chunk(b, 0, 0, 2)

    ring_copies, core_copies = ([], []), ([], [])

    def start_ring(b, dy, way, first=0, count=2):
        at = len(ring_copies[b])
        copy = remote(
            chunk(b, dy, first, count) if dy else mine(b), chunk(b, dy, first, count),
            ring_send.at[b, at], ring_recv.at[b, at], r, along[way % NY],
        )
        copy.start()
        ring_copies[b].append(copy)

    def start_core(b, dy, first=0, count=2):
        at = len(core_copies[b])
        copy = remote(
            chunk(b, dy, first, count) if dy else mine(b), chunk(b, dy, first, count),
            core_send.at[b, at], core_recv.at[b, at], r, other,
        )
        copy.start()
        core_copies[b].append(copy)

    own_hub = pltpu.make_async_copy(hub_got, chunk(HUB_ITEM, 0, 0, 2), load_sem.at[2])
    to_scalar = pltpu.make_async_copy(picks_got, picks_at, scalar_sem.at[1])

    def spread(b):
        if b == HUB_ITEM:

            def wait_hub(i, carry):
                hub_copy(i).wait()
                return carry

            lax.fori_loop(1 - c, CLASS, wait_hub, 0)
        else:
            far_copy.wait()
        for way in (2, -2, 1, -1):
            start_ring(b, 0, way)
        start_core(b, 0)
        if b == HUB_ITEM:
            own_hub.start()
        else:
            pick_copy.wait()
            to_scalar.start()

    def spread_on(b):
        for at, way in enumerate((2, -2)):
            ring_copies[b][at].wait_recv()
            on = way // 2
            start_ring(b, -way % NY, way, 0 if on > 0 else 1, 1)
            start_ring(b, -way % NY, on)
            start_core(b, -way % NY)
        for at, way in ((2, 1), (3, -1)):
            ring_copies[b][at].wait_recv()
            start_core(b, -way % NY)

    def collect(b):
        for at, way in ((5, 3), (7, -3)):
            ring_copies[b][at].wait_recv()
            start_core(b, -way % NY)
        for at, first in ((4, 0), (6, 1)):
            ring_copies[b][at].wait_recv()
            start_core(b, NY // 2, first, 1)
        for copy in core_copies[b]:
            copy.wait()

    last_copy = ([], [])

    def pass_on():
        to_scalar.wait()
        z_from = layer[NZ - FAR]
        group, odd = lax.div(z_from, 2), lax.rem(z_from, 2)
        for k, dx in enumerate(LINE):
            at = first_row[0] + line[dx]
            pair = halves(far[picks_at[0, at]], far[picks_at[1, at]])
            for h in range(2):
                if dx == 0:
                    source[h][4 + group, odd, x] = pair[h]
                    continue
                far_out[h, k] = pair[h]
                last_copy[h].append(remote(
                    far_out.at[h, k], source[h].at[4 + group, odd, x],
                    last_send.at[h, k], last_recv.at[h, k], first_row[0] + line[dx], q,
                ))
        for h in range(2):
            for copy in last_copy[h]:
                copy.start()

    spread(FAR_ITEM)
    spread(HUB_ITEM)
    second_half(0, 6)
    spread_on(FAR_ITEM)
    spread_on(HUB_ITEM)
    second_half(6, 14)
    collect(FAR_ITEM)
    pass_on()
    collect(HUB_ITEM)
    own_hub.wait()
    second_half(14, NEAR - 1)
    to_links.wait()
    load_tiles.wait()
    sums[EMPTY] = jnp.zeros((TILE, F), jnp.float32)
    source_1[pl.ds(0, 4)] = source_0[pl.ds(0, 4)]

    left = lax.broadcasted_iota(jnp.int32, (TILE, F), 1) < HALF

    def products(h):
        def step(n, carry):
            for u in range(UNROLL):
                k = n * UNROLL + u
                at = slots[0, 0, k]
                is_hub = at < HUBS
                tile = jnp.where(is_hub, at, lax.div(at + HUBS, 2))
                side = jnp.where(is_hub, h, lax.rem(at, 2))
                product = jnp.dot(
                    tiles[k],
                    source[h][lax.div(tile, 8), lax.rem(lax.div(tile, 4), 2), lax.rem(tile, 4)],
                    preferred_element_type=jnp.float32,
                )
                turned = jnp.concatenate([product[:, HALF:], product[:, :HALF]], axis=1)
                same = side == lax.rem(rows_at[0, 0, k], 2)
                sums[k] = sums[links[0, k]] + jnp.where(same, product, turned)
            return carry

        lax.fori_loop(0, KT // UNROLL, step, 0)

    cross_copy = ([], [])
    sum_copy = ([], [])

    def start_sums(h):
        def packed(rep):
            at = rep * 2
            return jnp.where(left, sums[links[1, at]], sums[links[1, at + 1]])

        for dy in ORDER:
            part_other[h, dy] = packed(along[dy] + 1 - 2 * c)
            copy = remote(
                part_other.at[h, dy], core_got.at[h, dy],
                cross_send.at[h, dy], cross_recv.at[h, dy], r, other,
            )
            copy.start()
            cross_copy[h].append(copy)
            part_own[h, dy] = packed(along[dy])
        for k, dy in enumerate(ORDER):
            cross_copy[h][k].wait_recv()
            if dy == 0:
                continue
            sum_out[h, dy] = (part_own[h, dy] + core_got[h, dy]).astype(jnp.bfloat16)
            copy = remote(
                sum_out.at[h, dy], sum_got.at[h, dy],
                sum_send.at[h, dy], sum_recv.at[h, dy], r, along[dy],
            )
            copy.start()
            sum_copy[h].append(copy)

    for h in range(2):
        for copy in near_copy[h] + last_copy[h]:
            copy.wait_recv()
        products(h)
        start_sums(h)

    totals = []
    for h in range(2):
        total = part_own[h, 0] + core_got[h, 0]
        for copy in sum_copy[h]:
            copy.wait_recv()
        for dy in range(1, NY):
            total = total + sum_got[h, dy].astype(jnp.float32)
        totals.append(total)
    for t, rows in enumerate(halves(*totals)):
        mixed = jnp.dot(rows.astype(jnp.bfloat16), weight[...], preferred_element_type=jnp.float32)
        out[pl.ds(t * TILE, TILE), :] = jnp.maximum(mixed + bias[...], 0.0).astype(jnp.bfloat16)

    for copy in [*near_copy[1], *ring_copies[0], *ring_copies[1], *last_copy[0], *last_copy[1]]:
        copy.wait_send()
    for copy in [*cross_copy[0], *cross_copy[1], *sum_copy[0], *sum_copy[1]]:
        copy.wait_send()


def local(features, hub_local, send_local, tile_rows, tile_slots, tile_values, weight, out_bias):
    dma = pltpu.SemaphoreType.DMA
    smem, vmem, anywhere = (
        pl.BlockSpec(memory_space=space) for space in (pltpu.SMEM, VMEM, pl.ANY)
    )
    bf16, f32, i32 = jnp.bfloat16, jnp.float32, jnp.int32
    picks = send_local[0, 0].T
    rows_in = tile_rows.reshape(1, KT)
    return pl.pallas_call(
        layer_kernel,
        out_shape=jax.ShapeDtypeStruct((SHARE, F), bf16),
        in_specs=[anywhere, smem, smem, vmem, smem, vmem, smem, anywhere, vmem, vmem],
        out_specs=vmem,
        scratch_shapes=[
            VMEM((ROWS, TILE, F), bf16),
            VMEM((KT, TILE, TILE), bf16),
            VMEM((NEAR, 2, TILE, F), bf16),
            VMEM((TILE, F), bf16),
            VMEM((4, 4, PIECE, F), bf16),
            VMEM((ROWS, TILE, F), bf16),
            VMEM((2, NX, TILE, F), bf16),
            VMEM((2, ROWS), i32),
            pltpu.SMEM((2, ROWS), i32),
            VMEM((8, 2, 4, TILE, F), bf16),
            VMEM((8, 2, 4, TILE, F), bf16),
            VMEM((8, 128), i32),
            pltpu.SMEM((8, 128), i32),
            VMEM((KT + 1, TILE, F), f32),
            VMEM((2, NY, TILE, F), f32),
            VMEM((2, NY, TILE, F), f32),
            VMEM((2, NY, TILE, F), f32),
            VMEM((2, NY, TILE, F), bf16),
            VMEM((2, NY, TILE, F), bf16),
            dma((3,)),
            dma((2,)),
            dma((2, NEAR)),
            dma((2, NEAR)),
            dma((CLASS,)),
            dma((CLASS,)),
            dma((2,)),
            dma((2,)),
            dma((2, 8)),
            dma((2, 8)),
            dma((2, 9)),
            dma((2, 9)),
            dma((2, NX)),
            dma((2, NX)),
            dma((2, NY)),
            dma((2, NY)),
            dma((2, NY)),
            dma((2, NY)),
        ],
        compiler_params=pltpu.CompilerParams(
            collective_id=0, has_side_effects=True, vmem_limit_bytes=56 * 1024 * 1024
        ),
        name="layer",
    )(
        features.reshape(ROWS, TILE, F), hub_local, picks, picks, tile_rows, rows_in,
        tile_slots, tile_values[0, 0], weight, out_bias.reshape(1, F),
    )


def solution(mesh):
    placed = (
        P("row", None),
        P("row", None),
        P("row", "rep", None, None),
        P("row", "rep", None),
        P("row", "rep", None),
        P("row", "rep", None, None, None),
        P(),
        P(),
    )
    return jax.shard_map(
        local, mesh=mesh, in_specs=placed, out_specs=P(("row", "rep"), None), check_vma=False
    )
```

```python
import functools

import jax
import jax.numpy as jnp
from jax import lax
from jax.experimental import pallas as pl
from jax.experimental.pallas import tpu as pltpu
from jax.sharding import PartitionSpec as P

F = 128
TILE = 128
NX = 4
NZ = 8
NY = 8
ROWS = 32
HUBS = 32
PIECE = 16
KT = 112
VMEM = pltpu.VMEM
MESH = pl.DeviceIdType.MESH


def zigzag(k, middle):
    return middle + (1 - 2 * (k % 2)) * ((k + 1) // 2)


FAR = (4, 3, 5)
LINE = (2, 1, 3, 0)
CLASS = 16
HUB_ITEM = len(FAR)
EMPTY = KT
SHARE = 256
HALF = F // 2
ORDER = tuple(zigzag(k, NY // 2) for k in range(NY))
UNROLL = 28


def halves(one, two):
    return (
        jnp.concatenate([one[:, :HALF], two[:, :HALF]], axis=1),
        jnp.concatenate([one[:, HALF:], two[:, HALF:]], axis=1),
    )


def layer_kernel(
    features, hub_in, picks_in, rows_in, slots_in, values, weight_in, bias_in, out,
    hub, picks, rows_at, rows_lane, slots, weight, bias, feat, tiles, out_0, out_1, hub_tile, hub_got, far_mine, far_0, far_1, far_2, far_out, picks_got, picks_at,
    source_0, source_1, linked, links, sums, part_own, part_other, core_got, sum_out, sum_got,
    load_sem, scalar_sem, near_send, near_recv, hub_send, hub_recv, far_send, far_recv,
    pick_send, pick_recv, ring_send, ring_recv, core_send, core_recv, last_send, last_recv,
    cross_send, cross_recv, sum_send, sum_recv,
):
    source = (source_0, source_1)
    far = (far_0, far_1, far_2)
    near_out = (out_0, out_1)
    r = lax.axis_index("row")
    q = lax.axis_index("rep")
    z, x = lax.div(r, NX), lax.rem(r, NX)
    y, c = lax.div(q, 2), lax.rem(q, 2)
    kind = lax.rem(z + c, 2)
    half_z, odd_z = lax.div(z, 2), lax.rem(z, 2)
    other = q + 1 - 2 * c
    layer = [z] + [lax.rem(z + d, NZ) for d in range(1, NZ)]
    line = [lax.rem(x + d, NX) for d in range(NX)]
    first_row = [at * NX for at in layer]
    place = [y] + [lax.rem(y + d, NY) for d in range(1, NY)]
    shares = [at * 2 + c for at in place]
    pieces = [pl.multiple_of(at * PIECE, PIECE) for at in place]
    along = [at * 2 + c for at in place]

    def remote(src, dst, send, recv, row, rep):
        return pltpu.make_async_remote_copy(
            src_ref=src, dst_ref=dst, send_sem=send, recv_sem=recv,
            device_id=(row, rep), device_id_type=MESH,
        )

    loads = {}
    for n, (name, src, dst) in enumerate((
        ("hub", hub_in, hub),
        ("picks", picks_in, picks),
        ("feat", features, feat),
        ("rows", rows_in, rows_at),
        ("lane", rows_in, rows_lane),
        ("slots", slots_in, slots),
        ("weight", weight_in, weight),
        ("bias", bias_in, bias),
        ("tiles", values, tiles),
    )):
        loads[name] = pltpu.make_async_copy(src, dst, load_sem.at[1 + n])
        loads[name].start()

    barrier = pltpu.get_barrier_semaphore()

    def greet(row, rep):
        pl.semaphore_signal(barrier, inc=1, device_id=(row, rep), device_id_type=MESH)

    for dz in range(NZ):
        for dx in range(NX):
            if dz or dx:
                greet(first_row[dz] + line[dx], q)
    for rep in (*along[1:], other):
        greet(r, rep)

    pl.semaphore_wait(barrier, ROWS - 1 + NY)

    for name in ("hub", "picks", "feat"):
        loads[name].wait()
    far_mine[...] = halves(feat[2 * shares[0]], feat[2 * shares[0] + 1])[1]
    far_copy, pick_copy = [], []
    for b, dz in enumerate(FAR):
        to = first_row[dz] + x
        far_copy.append(remote(
            far_mine, far[b].at[shares[0]], far_send.at[b], far_recv.at[b], to, q
        ))
        pick_copy.append(remote(
            picks_in, picks_got.at[b], pick_send.at[b], pick_recv.at[b], to, q
        ))
        far_copy[b].start()
        pick_copy[b].start()
    hub_tile[...] = feat[hub[0, 0]]

    @pl.when(c == 0)
    def _():
        hub_got[half_z, x] = hub_tile[pl.ds(pieces[0], PIECE), :]

    def hub_copy(i):
        row = lax.rem(z + 2 * lax.div(i, NX) + c, NZ) * NX + lax.rem(x + lax.rem(i, NX), NX)
        return remote(
            hub_tile.at[pl.ds(pieces[0], PIECE)], hub_got.at[half_z, x],
            hub_send.at[i], hub_recv.at[i], row, q,
        )

    def start_hub(i, carry):
        hub_copy(i).start()
        return carry

    lax.fori_loop(1 - c, CLASS, start_hub, 0)
    near_copy = ([], [])

    def first_half(dz):
        for dx in LINE:
            row = first_row[dz] + line[dx]
            pair = halves(feat[picks[0, row]], feat[picks[1, row]])
            for h in range(1 if dz in FAR else 2):
                at = source[h].at[4 + half_z, odd_z, x]
                if dz == 0 and dx == 0:
                    at[...] = pair[h]
                    continue
                i = len(near_copy[h])
                near_out[h][i] = pair[h]
                near_copy[h].append(remote(
                    near_out[h].at[i], at, near_send.at[h, i], near_recv.at[h, i], row, q
                ))
                if h == 0:
                    near_copy[0][i].start()

    def second_half(first, last):
        for i in range(first, last):
            near_copy[1][i].start()

    def chunk(b, dy, part):
        if b == HUB_ITEM:
            groups = (pl.ds(0, 4), pl.ds(0, 2), pl.ds(2, 2))[part]
            return source_0.at[groups, kind, :, pl.ds(pieces[dy], PIECE)]
        return far[b].at[shares[dy], (pl.ds(0, TILE), pl.ds(0, HALF), pl.ds(HALF, HALF))[part]]

    def mine(b):
        return hub_got if b == HUB_ITEM else chunk(b, 0, 0)

    ring_copies = [[] for _ in range(HUB_ITEM + 1)]
    core_copies = [[] for _ in range(HUB_ITEM + 1)]

    def start_ring(b, dy, way, part=0):
        at = len(ring_copies[b])
        copy = remote(
            chunk(b, dy, part) if dy else mine(b), chunk(b, dy, part),
            ring_send.at[b, at], ring_recv.at[b, at], r, along[way % NY],
        )
        copy.start()
        ring_copies[b].append(copy)

    def start_core(b, dy, part=0):
        at = len(core_copies[b])
        copy = remote(
            chunk(b, dy, part) if dy else mine(b), chunk(b, dy, part),
            core_send.at[b, at], core_recv.at[b, at], r, other,
        )
        copy.start()
        core_copies[b].append(copy)

    own_hub = pltpu.make_async_copy(hub_got, chunk(HUB_ITEM, 0, 0), load_sem.at[0])
    to_scalar = [
        pltpu.make_async_copy(picks_got.at[b], picks_at.at[b], scalar_sem.at[1 + b])
        for b in range(HUB_ITEM)
    ]

    def spread(b):
        if b == HUB_ITEM:

            def wait_hub(i, carry):
                hub_copy(i).wait()
                return carry

            lax.fori_loop(1 - c, CLASS, wait_hub, 0)
        else:
            far_copy[b].wait()
        for way in (2, -2, 1, -1):
            start_ring(b, 0, way)
        start_core(b, 0)
        if b == HUB_ITEM:
            own_hub.start()
        else:
            pick_copy[b].wait()
            to_scalar[b].start()

    def spread_on(b):
        for at, way in enumerate((2, -2)):
            ring_copies[b][at].wait_recv()
            on = way // 2
            start_ring(b, -way % NY, way, 1 if on > 0 else 2)
            start_ring(b, -way % NY, on)
            start_core(b, -way % NY)
        for at, way in ((2, 1), (3, -1)):
            ring_copies[b][at].wait_recv()
            start_core(b, -way % NY)

    def collect(b):
        for at, way in ((5, 3), (7, -3)):
            ring_copies[b][at].wait_recv()
            start_core(b, -way % NY)
        for at, part in ((4, 1), (6, 2)):
            ring_copies[b][at].wait_recv()
            start_core(b, NY // 2, part)
        for copy in core_copies[b]:
            copy.wait()

    last_copy = []

    def pass_on(b):
        to_scalar[b].wait()
        z_from = layer[NZ - FAR[b]]
        at = source_1.at[4 + lax.div(z_from, 2), lax.rem(z_from, 2), x]
        for k, dx in enumerate(LINE):
            row = first_row[0] + line[dx]
            sides = []
            for j in range(2):
                pick = picks_at[b, j, row]
                pair = far[b][lax.div(pick, 2)]
                turned = jnp.concatenate([pair[:, HALF:], pair[:, :HALF]], axis=1)
                sides.append(jnp.where(lax.rem(pick, 2) == j, pair, turned))
            both = jnp.concatenate([sides[0][:, :HALF], sides[1][:, HALF:]], axis=1)
            if dx == 0:
                at[...] = both
                continue
            far_out[b, k] = both
            copy = remote(
                far_out.at[b, k], at, last_send.at[b, k], last_recv.at[b, k], row, q
            )
            copy.start()
            last_copy.append(copy)

    first_half(2)
    first_half(6)
    spread(0)
    first_half(4)
    spread(HUB_ITEM)
    spread(1)
    spread(2)
    first_half(3)
    first_half(5)
    spread_on(0)
    spread_on(HUB_ITEM)
    first_half(1)
    first_half(7)
    first_half(0)
    spread_on(1)
    spread_on(2)
    second_half(0, len(near_copy[1]))
    collect(0)
    pass_on(0)
    collect(HUB_ITEM)
    own_hub.wait()

    lane = lax.broadcasted_iota(jnp.int32, (1, KT), 1)
    loads["rows"].wait()
    loads["lane"].wait()
    rows = rows_lane[...]

    def link(j, carry):
        before, final = carry
        row = rows_at[0, j]
        before = jnp.where((rows == row) & (lane > j), j, before)
        final = jnp.where(lane == row, j, final)
        return before, final

    none = jnp.full((1, KT), EMPTY, jnp.int32)
    before, final = lax.fori_loop(0, KT, link, (none, none))
    linked[...] = jnp.zeros((8, 128), jnp.int32)
    linked[pl.ds(0, 1), pl.ds(0, KT)] = before
    linked[pl.ds(1, 1), pl.ds(0, KT)] = final
    to_links = pltpu.make_async_copy(linked, links, scalar_sem.at[0])
    to_links.start()

    for b in (1, 2):
        collect(b)
        pass_on(b)
    to_links.wait()
    loads["slots"].wait()
    loads["tiles"].wait()
    sums[EMPTY] = jnp.zeros((TILE, F), jnp.float32)
    source_1[pl.ds(0, 4)] = source_0[pl.ds(0, 4)]

    left = lax.broadcasted_iota(jnp.int32, (TILE, F), 1) < HALF

    def products(h):
        def step(n, carry):
            for u in range(UNROLL):
                k = n * UNROLL + u
                at = slots[0, k]
                is_hub = at < HUBS
                tile = jnp.where(is_hub, at, lax.div(at + HUBS, 2))
                side = jnp.where(is_hub, h, lax.rem(at, 2))
                picked = source[h][lax.div(tile, 8), lax.rem(lax.div(tile, 4), 2), lax.rem(tile, 4)]
                turned = jnp.concatenate([picked[:, HALF:], picked[:, :HALF]], axis=1)
                same = side == lax.rem(rows_at[0, k], 2)
                sums[k] = sums[links[0, k]] + jnp.dot(
                    tiles[k], jnp.where(same, picked, turned), preferred_element_type=jnp.float32
                )
            return carry

        lax.fori_loop(0, KT // UNROLL, step, 0)

    cross_copy = ([], [])
    sum_copy = ([], [])

    def start_sums(h):
        def packed(rep):
            at = rep * 2
            return jnp.where(left, sums[links[1, at]], sums[links[1, at + 1]])

        for dy in ORDER:
            part_other[h, dy] = packed(along[dy] + 1 - 2 * c)
            copy = remote(
                part_other.at[h, dy], core_got.at[h, dy],
                cross_send.at[h, dy], cross_recv.at[h, dy], r, other,
            )
            copy.start()
            cross_copy[h].append(copy)
        for k, dy in enumerate(ORDER):
            own = packed(along[dy])
            cross_copy[h][k].wait_recv()
            if dy == 0:
                part_own[h] = own + core_got[h, dy]
                continue
            sum_out[h, dy] = (own + core_got[h, dy]).astype(jnp.bfloat16)
            copy = remote(
                sum_out.at[h, dy], sum_got.at[h, dy],
                sum_send.at[h, dy], sum_recv.at[h, dy], r, along[dy],
            )
            copy.start()
            sum_copy[h].append(copy)

    for h in range(2):
        for copy in near_copy[h] + (last_copy if h else []):
            copy.wait_recv()
        products(h)
        start_sums(h)

    totals = []
    loads["weight"].wait()
    loads["bias"].wait()
    for h in range(2):
        total = part_own[h]
        for copy, dy in zip(sum_copy[h], ORDER):
            copy.wait_recv()
            total = total + sum_got[h, dy].astype(jnp.float32)
        totals.append(total)
    for t, rows in enumerate(halves(*totals)):
        mixed = jnp.dot(rows.astype(jnp.bfloat16), weight[...], preferred_element_type=jnp.float32)
        out[pl.ds(t * TILE, TILE), :] = jnp.maximum(mixed + bias[...], 0.0).astype(jnp.bfloat16)

    for copy in [*near_copy[0], *near_copy[1], *last_copy]:
        copy.wait_send()
    for copies in ring_copies:
        for copy in copies:
            copy.wait_send()
    for copy in [*cross_copy[0], *cross_copy[1], *sum_copy[0], *sum_copy[1]]:
        copy.wait_send()


def local(features, hub_local, send_local, tile_rows, tile_slots, tile_values, weight, out_bias):
    dma = pltpu.SemaphoreType.DMA
    bf16, f32, i32 = jnp.bfloat16, jnp.float32, jnp.int32
    picks = send_local[0, 0].T
    rows_in = tile_rows.reshape(1, KT)
    return pl.pallas_call(
        layer_kernel,
        out_shape=jax.ShapeDtypeStruct((SHARE, F), bf16),
        in_specs=[pl.BlockSpec(memory_space=pltpu.HBM)] * 8,
        out_specs=pl.BlockSpec(memory_space=VMEM),
        scratch_shapes=[
            pltpu.SMEM((1, 1), i32),
            pltpu.SMEM((2, ROWS), i32),
            pltpu.SMEM((1, KT), i32),
            VMEM((1, KT), i32),
            pltpu.SMEM((1, KT), i32),
            VMEM((F, F), bf16),
            VMEM((1, F), f32),
            VMEM((ROWS, TILE, F), bf16),
            VMEM((KT, TILE, TILE), bf16),
            VMEM((ROWS - 1, TILE, F), bf16),
            VMEM((ROWS - 1, TILE, F), bf16),
            VMEM((TILE, F), bf16),
            VMEM((4, 4, PIECE, F), bf16),
            VMEM((TILE, F), bf16),
            *[VMEM((ROWS // 2, TILE, F), bf16)] * HUB_ITEM,
            VMEM((HUB_ITEM, NX, TILE, F), bf16),
            VMEM((HUB_ITEM, 2, ROWS), i32),
            pltpu.SMEM((HUB_ITEM, 2, ROWS), i32),
            VMEM((8, 2, 4, TILE, F), bf16),
            VMEM((8, 2, 4, TILE, F), bf16),
            VMEM((8, 128), i32),
            pltpu.SMEM((8, 128), i32),
            VMEM((KT + 1, TILE, F), f32),
            VMEM((2, TILE, F), f32),
            VMEM((2, NY, TILE, F), f32),
            VMEM((2, NY, TILE, F), f32),
            VMEM((2, NY, TILE, F), bf16),
            VMEM((2, NY, TILE, F), bf16),
            dma((10,)),
            dma((1 + HUB_ITEM,)),
            dma((2, ROWS)),
            dma((2, ROWS)),
            dma((CLASS,)),
            dma((CLASS,)),
            dma((HUB_ITEM,)),
            dma((HUB_ITEM,)),
            dma((HUB_ITEM,)),
            dma((HUB_ITEM,)),
            dma((HUB_ITEM + 1, 8)),
            dma((HUB_ITEM + 1, 8)),
            dma((HUB_ITEM + 1, 9)),
            dma((HUB_ITEM + 1, 9)),
            dma((HUB_ITEM, NX)),
            dma((HUB_ITEM, NX)),
            dma((2, NY)),
            dma((2, NY)),
            dma((2, NY)),
            dma((2, NY)),
        ],
        compiler_params=pltpu.CompilerParams(
            collective_id=0, has_side_effects=True, vmem_limit_bytes=56 * 1024 * 1024
        ),
        name="layer",
    )(
        features.reshape(ROWS, TILE, F), hub_local, picks, rows_in,
        tile_slots.reshape(1, KT), tile_values[0, 0], weight, out_bias.reshape(1, F),
    )


def solution(mesh):
    placed = (
        P("row", None),
        P("row", None),
        P("row", "rep", None, None),
        P("row", "rep", None),
        P("row", "rep", None),
        P("row", "rep", None, None, None),
        P(),
        P(),
    )
    return jax.shard_map(
        local, mesh=mesh, in_specs=placed, out_specs=P(("row", "rep"), None), check_vma=False
    )
```

```python
import functools

import jax
import jax.numpy as jnp
from jax import lax
from jax.experimental import pallas as pl
from jax.experimental.pallas import tpu as pltpu
from jax.sharding import PartitionSpec as P

F = 128
TILE = 128
NX = 4
NZ = 8
NY = 8
ROWS = 32
HUBS = 32
PIECE = 16
KT = 112
VMEM = pltpu.VMEM
MESH = pl.DeviceIdType.MESH


def zigzag(k, middle):
    return middle + (1 - 2 * (k % 2)) * ((k + 1) // 2)


FAR = (4, 3, 5)
LINE = (2, 1, 3, 0)
CLASS = 16
HUB_ITEM = len(FAR)
EMPTY = KT
SHARE = 256
HALF = F // 2
ORDER = tuple(zigzag(k, NY // 2) for k in range(NY))
UNROLL = 56


def halves(one, two):
    return (
        jnp.concatenate([one[:, :HALF], two[:, :HALF]], axis=1),
        jnp.concatenate([one[:, HALF:], two[:, HALF:]], axis=1),
    )


def layer_kernel(
    features, hub_in, picks_in, rows_in, slots_in, values, weight_in, bias_in, out,
    hub, picks, rows_at, rows_lane, slots, weight, bias, feat, tiles, out_0, out_1, hub_tile, hub_got, far_mine, far_0, far_1, far_2, far_out, picks_got, picks_at,
    source_0, source_1, linked, links, sums, part_own, part_other, core_got, sum_out, sum_got,
    load_sem, scalar_sem, near_send, near_recv, hub_send, hub_recv, far_send, far_recv,
    pick_send, pick_recv, ring_send, ring_recv, core_send, core_recv, last_send, last_recv,
    cross_send, cross_recv, sum_send, sum_recv,
):
    source = (source_0, source_1)
    far = (far_0, far_1, far_2)
    near_out = (out_0, out_1)
    r = lax.axis_index("row")
    q = lax.axis_index("rep")
    z, x = lax.div(r, NX), lax.rem(r, NX)
    y, c = lax.div(q, 2), lax.rem(q, 2)
    kind = lax.rem(z + c, 2)
    half_z, odd_z = lax.div(z, 2), lax.rem(z, 2)
    other = q + 1 - 2 * c
    layer = [z] + [lax.rem(z + d, NZ) for d in range(1, NZ)]
    line = [lax.rem(x + d, NX) for d in range(NX)]
    first_row = [at * NX for at in layer]
    place = [y] + [lax.rem(y + d, NY) for d in range(1, NY)]
    shares = [at * 2 + c for at in place]
    pieces = [pl.multiple_of(at * PIECE, PIECE) for at in place]
    along = [at * 2 + c for at in place]

    def remote(src, dst, send, recv, row, rep):
        return pltpu.make_async_remote_copy(
            src_ref=src, dst_ref=dst, send_sem=send, recv_sem=recv,
            device_id=(row, rep), device_id_type=MESH,
        )

    loads = {}
    for n, (name, src, dst) in enumerate((
        ("hub", hub_in, hub),
        ("picks", picks_in, picks),
        ("feat", features, feat),
        ("rows", rows_in, rows_at),
        ("lane", rows_in, rows_lane),
        ("slots", slots_in, slots),
        ("weight", weight_in, weight),
        ("bias", bias_in, bias),
        ("tiles", values, tiles),
    )):
        loads[name] = pltpu.make_async_copy(src, dst, load_sem.at[1 + n])
        loads[name].start()

    barrier = pltpu.get_barrier_semaphore()

    def greet(row, rep):
        pl.semaphore_signal(barrier, inc=1, device_id=(row, rep), device_id_type=MESH)

    for dz in range(NZ):
        for dx in range(NX):
            if dz or dx:
                greet(first_row[dz] + line[dx], q)
    for rep in (*along[1:], other):
        greet(r, rep)

    pl.semaphore_wait(barrier, ROWS - 1 + NY)

    for name in ("hub", "picks", "feat"):
        loads[name].wait()
    far_mine[...] = halves(feat[2 * shares[0]], feat[2 * shares[0] + 1])[1]
    far_copy, pick_copy = [], []
    for b, dz in enumerate(FAR):
        to = first_row[dz] + x
        far_copy.append(remote(
            far_mine, far[b].at[shares[0]], far_send.at[b], far_recv.at[b], to, q
        ))
        pick_copy.append(remote(
            picks_in, picks_got.at[b], pick_send.at[b], pick_recv.at[b], to, q
        ))
        far_copy[b].start()
        pick_copy[b].start()
    hub_tile[...] = feat[hub[0, 0]]

    @pl.when(c == 0)
    def _():
        hub_got[half_z, x] = hub_tile[pl.ds(pieces[0], PIECE), :]

    def hub_copy(i):
        row = lax.rem(z + 2 * lax.div(i, NX) + c, NZ) * NX + lax.rem(x + lax.rem(i, NX), NX)
        return remote(
            hub_tile.at[pl.ds(pieces[0], PIECE)], hub_got.at[half_z, x],
            hub_send.at[i], hub_recv.at[i], row, q,
        )

    def start_hub(i, carry):
        hub_copy(i).start()
        return carry

    lax.fori_loop(1 - c, CLASS, start_hub, 0)
    near_copy = ([], [])

    def first_half(dz):
        for dx in LINE:
            row = first_row[dz] + line[dx]
            pair = halves(feat[picks[0, row]], feat[picks[1, row]])
            for h in range(1 if dz in FAR else 2):
                at = source[h].at[4 + half_z, odd_z, x]
                if dz == 0 and dx == 0:
                    at[...] = pair[h]
                    continue
                i = len(near_copy[h])
                near_out[h][i] = pair[h]
                near_copy[h].append(remote(
                    near_out[h].at[i], at, near_send.at[h, i], near_recv.at[h, i], row, q
                ))
                if h == 0:
                    near_copy[0][i].start()

    def second_half(first, last):
        for i in range(first, last):
            near_copy[1][i].start()

    def chunk(b, dy, part):
        if b == HUB_ITEM:
            groups = (pl.ds(0, 4), pl.ds(0, 2), pl.ds(2, 2))[part]
            return source_0.at[groups, kind, :, pl.ds(pieces[dy], PIECE)]
        return far[b].at[shares[dy], (pl.ds(0, TILE), pl.ds(0, HALF), pl.ds(HALF, HALF))[part]]

    def mine(b):
        return hub_got if b == HUB_ITEM else chunk(b, 0, 0)

    ring_copies = [[] for _ in range(HUB_ITEM + 1)]
    core_copies = [[] for _ in range(HUB_ITEM + 1)]

    def start_ring(b, dy, way, part=0):
        at = len(ring_copies[b])
        copy = remote(
            chunk(b, dy, part) if dy else mine(b), chunk(b, dy, part),
            ring_send.at[b, at], ring_recv.at[b, at], r, along[way % NY],
        )
        copy.start()
        ring_copies[b].append(copy)

    def start_core(b, dy, part=0):
        at = len(core_copies[b])
        copy = remote(
            chunk(b, dy, part) if dy else mine(b), chunk(b, dy, part),
            core_send.at[b, at], core_recv.at[b, at], r, other,
        )
        copy.start()
        core_copies[b].append(copy)

    own_hub = pltpu.make_async_copy(hub_got, chunk(HUB_ITEM, 0, 0), load_sem.at[0])
    to_scalar = [
        pltpu.make_async_copy(picks_got.at[b], picks_at.at[b], scalar_sem.at[1 + b])
        for b in range(HUB_ITEM)
    ]

    def spread(b):
        if b == HUB_ITEM:

            def wait_hub(i, carry):
                hub_copy(i).wait()
                return carry

            lax.fori_loop(1 - c, CLASS, wait_hub, 0)
        else:
            far_copy[b].wait()
        for way in (2, -2, 1, -1):
            start_ring(b, 0, way)
        start_core(b, 0)
        if b == HUB_ITEM:
            own_hub.start()
        else:
            pick_copy[b].wait()
            to_scalar[b].start()

    def spread_on(b):
        for at, way in enumerate((2, -2)):
            ring_copies[b][at].wait_recv()
            on = way // 2
            start_ring(b, -way % NY, way, 1 if on > 0 else 2)
            start_ring(b, -way % NY, on)
            start_core(b, -way % NY)
        for at, way in ((2, 1), (3, -1)):
            ring_copies[b][at].wait_recv()
            start_core(b, -way % NY)

    def collect(b):
        for at, way in ((5, 3), (7, -3)):
            ring_copies[b][at].wait_recv()
            start_core(b, -way % NY)
        for at, part in ((4, 1), (6, 2)):
            ring_copies[b][at].wait_recv()
            start_core(b, NY // 2, part)
        for copy in core_copies[b]:
            copy.wait()

    last_copy = []

    def pass_on(b):
        to_scalar[b].wait()
        z_from = layer[NZ - FAR[b]]
        at = source_1.at[4 + lax.div(z_from, 2), lax.rem(z_from, 2), x]
        for k, dx in enumerate(LINE):
            row = first_row[0] + line[dx]
            sides = []
            for j in range(2):
                pick = picks_at[b, j, row]
                pair = far[b][lax.div(pick, 2)]
                turned = jnp.concatenate([pair[:, HALF:], pair[:, :HALF]], axis=1)
                sides.append(jnp.where(lax.rem(pick, 2) == j, pair, turned))
            both = jnp.concatenate([sides[0][:, :HALF], sides[1][:, HALF:]], axis=1)
            if dx == 0:
                at[...] = both
                continue
            far_out[b, k] = both
            copy = remote(
                far_out.at[b, k], at, last_send.at[b, k], last_recv.at[b, k], row, q
            )
            copy.start()
            last_copy.append(copy)

    first_half(2)
    first_half(6)
    spread(0)
    first_half(4)
    spread(HUB_ITEM)
    spread(1)
    spread(2)
    first_half(3)
    first_half(5)
    spread_on(0)
    spread_on(HUB_ITEM)
    first_half(1)
    first_half(7)
    first_half(0)
    spread_on(1)
    spread_on(2)
    second_half(0, len(near_copy[1]))
    collect(0)
    pass_on(0)
    collect(HUB_ITEM)
    own_hub.wait()

    lane = lax.broadcasted_iota(jnp.int32, (1, KT), 1)
    loads["rows"].wait()
    loads["lane"].wait()
    rows = rows_lane[...]

    def link(j, carry):
        before, final = carry
        row = rows_at[0, j]
        before = jnp.where((rows == row) & (lane > j), j, before)
        final = jnp.where(lane == row, j, final)
        return before, final

    none = jnp.full((1, KT), EMPTY, jnp.int32)
    before, final = lax.fori_loop(0, KT, link, (none, none))
    linked[...] = jnp.zeros((8, 128), jnp.int32)
    linked[pl.ds(0, 1), pl.ds(0, KT)] = before
    linked[pl.ds(1, 1), pl.ds(0, KT)] = final
    to_links = pltpu.make_async_copy(linked, links, scalar_sem.at[0])
    to_links.start()

    for b in (1, 2):
        collect(b)
        pass_on(b)
    to_links.wait()
    loads["slots"].wait()
    loads["tiles"].wait()
    sums[EMPTY] = jnp.zeros((TILE, F), jnp.float32)
    source_1[pl.ds(0, 4)] = source_0[pl.ds(0, 4)]

    left = lax.broadcasted_iota(jnp.int32, (TILE, F), 1) < HALF

    def products(h):
        def step(n, carry):
            for u in range(UNROLL):
                k = n * UNROLL + u
                at = slots[0, k]
                is_hub = at < HUBS
                tile = jnp.where(is_hub, at, lax.div(at + HUBS, 2))
                side = jnp.where(is_hub, h, lax.rem(at, 2))
                picked = source[h][lax.div(tile, 8), lax.rem(lax.div(tile, 4), 2), lax.rem(tile, 4)]
                turned = jnp.concatenate([picked[:, HALF:], picked[:, :HALF]], axis=1)
                same = side == lax.rem(rows_at[0, k], 2)
                sums[k] = sums[links[0, k]] + jnp.dot(
                    tiles[k], jnp.where(same, picked, turned), preferred_element_type=jnp.float32
                )
            return carry

        lax.fori_loop(0, KT // UNROLL, step, 0)

    cross_copy = ([], [])
    sum_copy = ([], [])

    def start_sums(h):
        def packed(rep):
            at = rep * 2
            return jnp.where(left, sums[links[1, at]], sums[links[1, at + 1]])

        for dy in ORDER:
            part_other[h, dy] = packed(along[dy] + 1 - 2 * c)
            copy = remote(
                part_other.at[h, dy], core_got.at[h, dy],
                cross_send.at[h, dy], cross_recv.at[h, dy], r, other,
            )
            copy.start()
            cross_copy[h].append(copy)
        for k, dy in enumerate(ORDER):
            own = packed(along[dy])
            cross_copy[h][k].wait_recv()
            if dy == 0:
                part_own[h] = own + core_got[h, dy]
                continue
            sum_out[h, dy] = (own + core_got[h, dy]).astype(jnp.bfloat16)
            copy = remote(
                sum_out.at[h, dy], sum_got.at[h, dy],
                sum_send.at[h, dy], sum_recv.at[h, dy], r, along[dy],
            )
            copy.start()
            sum_copy[h].append(copy)

    for h in range(2):
        for copy in near_copy[h] + (last_copy if h else []):
            copy.wait_recv()
        products(h)
        start_sums(h)

    totals = []
    loads["weight"].wait()
    loads["bias"].wait()
    for h in range(2):
        total = part_own[h]
        for copy, dy in zip(sum_copy[h], ORDER):
            copy.wait_recv()
            total = total + sum_got[h, dy].astype(jnp.float32)
        totals.append(total)
    for t, rows in enumerate(halves(*totals)):
        mixed = jnp.dot(rows.astype(jnp.bfloat16), weight[...], preferred_element_type=jnp.float32)
        out[pl.ds(t * TILE, TILE), :] = jnp.maximum(mixed + bias[...], 0.0).astype(jnp.bfloat16)

    for copy in [*near_copy[0], *near_copy[1], *last_copy]:
        copy.wait_send()
    for copies in ring_copies:
        for copy in copies:
            copy.wait_send()
    for copy in [*cross_copy[0], *cross_copy[1], *sum_copy[0], *sum_copy[1]]:
        copy.wait_send()


def local(features, hub_local, send_local, tile_rows, tile_slots, tile_values, weight, out_bias):
    dma = pltpu.SemaphoreType.DMA
    bf16, f32, i32 = jnp.bfloat16, jnp.float32, jnp.int32
    picks = send_local[0, 0].T
    rows_in = tile_rows.reshape(1, KT)
    return pl.pallas_call(
        layer_kernel,
        out_shape=jax.ShapeDtypeStruct((SHARE, F), bf16),
        in_specs=[pl.BlockSpec(memory_space=pltpu.HBM)] * 8,
        out_specs=pl.BlockSpec(memory_space=VMEM),
        scratch_shapes=[
            pltpu.SMEM((1, 1), i32),
            pltpu.SMEM((2, ROWS), i32),
            pltpu.SMEM((1, KT), i32),
            VMEM((1, KT), i32),
            pltpu.SMEM((1, KT), i32),
            VMEM((F, F), bf16),
            VMEM((1, F), f32),
            VMEM((ROWS, TILE, F), bf16),
            VMEM((KT, TILE, TILE), bf16),
            VMEM((ROWS - 1, TILE, F), bf16),
            VMEM((ROWS - 1, TILE, F), bf16),
            VMEM((TILE, F), bf16),
            VMEM((4, 4, PIECE, F), bf16),
            VMEM((TILE, F), bf16),
            *[VMEM((ROWS // 2, TILE, F), bf16)] * HUB_ITEM,
            VMEM((HUB_ITEM, NX, TILE, F), bf16),
            VMEM((HUB_ITEM, 2, ROWS), i32),
            pltpu.SMEM((HUB_ITEM, 2, ROWS), i32),
            VMEM((8, 2, 4, TILE, F), bf16),
            VMEM((8, 2, 4, TILE, F), bf16),
            VMEM((8, 128), i32),
            pltpu.SMEM((8, 128), i32),
            VMEM((KT + 1, TILE, F), f32),
            VMEM((2, TILE, F), f32),
            VMEM((2, NY, TILE, F), f32),
            VMEM((2, NY, TILE, F), f32),
            VMEM((2, NY, TILE, F), bf16),
            VMEM((2, NY, TILE, F), bf16),
            dma((10,)),
            dma((1 + HUB_ITEM,)),
            dma((2, ROWS)),
            dma((2, ROWS)),
            dma((CLASS,)),
            dma((CLASS,)),
            dma((HUB_ITEM,)),
            dma((HUB_ITEM,)),
            dma((HUB_ITEM,)),
            dma((HUB_ITEM,)),
            dma((HUB_ITEM + 1, 8)),
            dma((HUB_ITEM + 1, 8)),
            dma((HUB_ITEM + 1, 9)),
            dma((HUB_ITEM + 1, 9)),
            dma((HUB_ITEM, NX)),
            dma((HUB_ITEM, NX)),
            dma((2, NY)),
            dma((2, NY)),
            dma((2, NY)),
            dma((2, NY)),
        ],
        compiler_params=pltpu.CompilerParams(
            collective_id=0, has_side_effects=True, vmem_limit_bytes=56 * 1024 * 1024
        ),
        name="layer",
    )(
        features.reshape(ROWS, TILE, F), hub_local, picks, rows_in,
        tile_slots.reshape(1, KT), tile_values[0, 0], weight, out_bias.reshape(1, F),
    )


def solution(mesh):
    placed = (
        P("row", None),
        P("row", None),
        P("row", "rep", None, None),
        P("row", "rep", None),
        P("row", "rep", None),
        P("row", "rep", None, None, None),
        P(),
        P(),
    )
    return jax.shard_map(
        local, mesh=mesh, in_specs=placed, out_specs=P(("row", "rep"), None), check_vma=False
    )
```
